32 devices in a mesh: parts: 2 (over x), pos: 8 (over z, y), slab: 2 (over core).
Axes of the slice: x: 2, y: 2, z: 4, core: 2. Of those that a mesh axis runs over, the one named last changes fastest.
Arguments:
- obj_real: float32 [8, 2048, 1024], P(('parts', 'slab'), 'pos'), parts along dimension 0, may hold values from 0.5 to 1.5
- obj_imag: float32 [8, 2048, 1024], P(('parts', 'slab'), 'pos'), parts along dimension 0, may hold values from -1.5 to 1.5
- probe: float32 [2, 256, 256], replicated, may hold values from -5 to 5
- taps: float32 [2, 63], replicated, may hold values from -1.3 to 1.3
- intensity: float32 [32, 256, 256], P(('parts', 'pos')), parts along dimension 0, may hold values from 0.25 to 8
- row_off: int32 [32], P(('parts', 'pos')), parts along dimension 0, may hold values from 0 to 255
- col_off: int32 [32], P(('parts', 'pos')), parts along dimension 0, may hold values from 0 to 768
Outputs:
- grad_real: float32 [8, 2048, 1024], P(('parts', 'slab'), 'pos'), parts along dimension 0
- grad_imag: float32 [8, 2048, 1024], P(('parts', 'slab'), 'pos'), parts along dimension 0
The draws below stay inside these ranges and needn't reach their ends.
There are 2 independent parts, one for each index of `parts`. The reference program is written for one: setup_inputs(seed, part) draws one part's arguments, and reference() takes and returns one part's arrays. A program takes and returns all parts, laid end to end along the dimension named above; an argument that names none is the same for every part. Nothing has to cross between parts.
All inputs are finite; a program needn't handle non-finite values.
Results may differ from the reference program's by a relative error of at most 0.0003.
Values sent between devices are 32-bit elements; how exact they have to be, the bound alone decides.
A program may use at most 128 MiB of HBM per device.

```python
import math
import jax
import jax.numpy as jnp
from jax import lax

PROBE = 256
TAPS = 63
POSITIONS_LOCAL = 2
OBJ_COLS = 1024
SLICES = 4
POSITIONS = 16
OBJ_ROWS = 2048
N_POS = 8


def draw_taps(key, part):
    phase_key = jax.random.fold_in(key, 11)
    size_key = jax.random.fold_in(key, 12)
    half = (TAPS - 1) // 2
    offsets = jnp.arange(TAPS, dtype=jnp.float32) - float(half)
    chirp = math.pi / TAPS * offsets * offsets
    jitter = jax.random.uniform(phase_key, (TAPS,), jnp.float32, -0.3, 0.3)
    amplitude = jax.random.uniform(size_key, (TAPS,), jnp.float32, 0.9, 1.1)
    angle = chirp + jitter
    scale = amplitude / math.sqrt(TAPS)
    return jnp.stack([scale * jnp.cos(angle), scale * jnp.sin(angle)], 0).astype(jnp.float32)


def place_ends(entries, key, low, top_value):
    shape = entries.shape
    spot = [jax.random.randint(jax.random.fold_in(key, axis), (), 0, shape[axis]) for axis in range(len(shape))]
    entries = entries.at[tuple(spot)].set(low)
    longest = shape.index(max(shape))
    spot[longest] = (spot[longest] + 1) % shape[longest]
    return entries.at[tuple(spot)].set(top_value)


def steps_of(stream_key, dims, split, low, largest):
    loudness, own = 1.0, jax.random.fold_in(stream_key, 6)
    for axis_at, parts in split:
        heights = jnp.exp(jax.random.uniform(jax.random.fold_in(own, axis_at), (parts,), jnp.float32, low / len(split), largest / len(split)))
        loudness = loudness * jnp.repeat(heights, dims[axis_at] // parts).reshape([-1 if axis == axis_at else 1 for axis in range(len(dims))])
    return loudness


def centred(own_key, dims, deviation, bound, cuts=(), held_as=jnp.bfloat16):
    values = jax.random.normal(own_key, dims, jnp.float32) * deviation
    if len(cuts) > 0:
        values = steps_of(own_key, dims, cuts, -0.22, 0.18) * values
    return jnp.clip(values, min=-bound, max=bound).astype(held_as)


def setup_inputs(seed: int = 0, part: int = 0) -> dict:
    keys = jax.random.split(jax.random.key(seed), 8)
    part_keys = jax.random.split(jax.random.fold_in(keys[7], part), 8)
    return {
        "obj_real": jnp.clip(1.0 + 0.1 * jax.random.normal(part_keys[0], (SLICES, OBJ_ROWS, OBJ_COLS), jnp.float32), 0.5, 1.5),
        "obj_imag": centred(part_keys[1], (SLICES, OBJ_ROWS, OBJ_COLS), 0.3, 1.5, ((0, 2), (1, 8)), jnp.float32),
        "probe": centred(keys[2], (2, PROBE, PROBE), 1.0, 5.0, (), jnp.float32),
        "taps": draw_taps(jax.random.fold_in(keys[7], 71), part),
        "intensity": jnp.clip(jnp.exp(math.log(8.0) - 3.465736 * jax.random.uniform(part_keys[4], (POSITIONS, PROBE, PROBE), jnp.float32) ** steps_of(part_keys[4], (POSITIONS, PROBE, PROBE), ((0, 8),), -0.2, 0.2)), 0.25, 8.0),
        "row_off": place_ends(jax.random.randint(part_keys[5], (POSITIONS,), 0, PROBE), jax.random.fold_in(part_keys[5], 1), 0, PROBE - 1).astype(jnp.int32),
        "col_off": place_ends(jax.random.randint(part_keys[6], (POSITIONS,), 0, OBJ_COLS - PROBE + 1), jax.random.fold_in(part_keys[6], 1), 0, OBJ_COLS - PROBE).astype(jnp.int32),
    }


HIGH = lax.Precision.HIGHEST

def cprod(form, ar, ai, br, bi):

    def mul(left, right):
        return jnp.einsum(form, left, right, precision=HIGH, preferred_element_type=jnp.float32)
    return (mul(ar, br) - mul(ai, bi), mul(ar, bi) + mul(ai, br))

def band(taps, width):
    rows = jnp.arange(width, dtype=jnp.int32)[:, None]
    cols = jnp.arange(width, dtype=jnp.int32)[None, :]
    offset = cols - rows
    half = (taps.shape[1] - 1) // 2
    index = jnp.clip(offset + half, 0, taps.shape[1] - 1)
    inside = jnp.abs(offset) <= half
    return (jnp.where(inside, taps[0][index], 0.0), jnp.where(inside, taps[1][index], 0.0))

def fourier(width):
    steps = jnp.arange(width, dtype=jnp.int32)
    phase = steps[:, None] * steps[None, :] % width
    angle = 2.0 * math.pi / width * phase.astype(jnp.float32)
    norm = 1.0 / math.sqrt(width)
    return (jnp.cos(angle) * norm, -jnp.sin(angle) * norm)

def propagate(kr, ki, xr, xi):
    left = cprod('ij,bjk->bik', kr, ki, xr, xi)
    return cprod('bij,kj->bik', left[0], left[1], kr, ki)

def adjoint_prop(kr, ki, xr, xi):
    left = cprod('ji,bjk->bik', kr, -ki, xr, xi)
    return cprod('bij,jk->bik', left[0], left[1], kr, -ki)

def target_amplitude(exit_wave_real, exit_wave_imaginary, measured_pattern, wave_real, wave_imaginary):
    left = cprod('ij,bjk->bik', wave_real, wave_imaginary, exit_wave_real, exit_wave_imaginary)
    farfield_real, farfield_imaginary = cprod('bij,jk->bik', left[0], left[1], wave_real, wave_imaginary)
    amplitude_residual = farfield_real * farfield_real + farfield_imaginary * farfield_imaginary - measured_pattern
    grad_r = 2.0 * amplitude_residual * farfield_real
    grad_i = 2.0 * amplitude_residual * farfield_imaginary
    back = cprod('ij,bjk->bik', wave_real, -wave_imaginary, grad_r, grad_i)
    return cprod('bij,jk->bik', back[0], back[1], wave_real, -wave_imaginary)

def cut(ext_r, ext_i, rows, cols, width):
    depth = ext_r.shape[0]
    zero = jnp.zeros((), jnp.int32)

    def one(row, col):
        start = (zero, row, col)
        return (lax.dynamic_slice(ext_r, start, (depth, width, width)), lax.dynamic_slice(ext_i, start, (depth, width, width)))
    return jax.vmap(one)(rows, cols)

def forward_pass(src_r, src_i, pat_r, pat_i, kr, ki):
    waves_r, waves_i = ([], [])
    cur_r, cur_i = (src_r, src_i)
    for level in range(pat_r.shape[1]):
        waves_r.append(cur_r)
        waves_i.append(cur_i)
        o_r = pat_r[:, level]
        o_i = pat_i[:, level]
        cur_r, cur_i = propagate(kr, ki, cur_r * o_r - cur_i * o_i, cur_r * o_i + cur_i * o_r)
    return (jnp.stack(waves_r, 1), jnp.stack(waves_i, 1), cur_r, cur_i)

def backward_pass(chirp_real, chirp_imaginary, waves_r, waves_i, pat_r, pat_i, kr, ki):
    depth = pat_r.shape[1]
    terms_r = [None] * depth
    terms_i = [None] * depth
    for level in reversed(range(depth)):
        a_r, a_i = adjoint_prop(kr, ki, chirp_real, chirp_imaginary)
        w_r = waves_r[:, level]
        w_i = waves_i[:, level]
        terms_r[level] = a_r * w_r + a_i * w_i
        terms_i[level] = a_i * w_r - a_r * w_i
        o_r = pat_r[:, level]
        o_i = pat_i[:, level]
        chirp_real, chirp_imaginary = (a_r * o_r + a_i * o_i, a_i * o_r - a_r * o_i)
    return (chirp_real, chirp_imaginary, jnp.stack(terms_r, 1), jnp.stack(terms_i, 1))

def deposit(acc_r, acc_i, term_r, term_i, rows, cols):
    depth, width = (term_r.shape[1], term_r.shape[2])
    zero = jnp.zeros((), jnp.int32)

    def add_one(item, state):
        total_r, total_i = state
        start = (zero, rows[item], cols[item])
        now_r = lax.dynamic_slice(total_r, start, (depth, width, width))
        now_i = lax.dynamic_slice(total_i, start, (depth, width, width))
        total_r = lax.dynamic_update_slice(total_r, now_r + term_r[item], start)
        total_i = lax.dynamic_update_slice(total_i, now_i + term_i[item], start)
        return (total_r, total_i)
    return lax.fori_loop(0, term_r.shape[0], add_one, (acc_r, acc_i))

def reference(obj_real, obj_imag, probe, taps, intensity, row_off, col_off):
    width = PROBE
    kr, ki = band(taps, width)
    wave_real, wave_imaginary = fourier(width)
    ext_r = jnp.concatenate([obj_real, obj_real[:, :width]], axis=1)
    ext_i = jnp.concatenate([obj_imag, obj_imag[:, :width]], axis=1)
    lead_r = jnp.broadcast_to(probe[0], (POSITIONS_LOCAL, width, width))
    lead_i = jnp.broadcast_to(probe[1], (POSITIONS_LOCAL, width, width))

    def group(acc, index):
        first_slice_flag = (index * POSITIONS_LOCAL).astype(jnp.int32)
        rows = index.astype(jnp.int32) * width + lax.dynamic_slice_in_dim(row_off, first_slice_flag, POSITIONS_LOCAL, 0)
        cols = lax.dynamic_slice_in_dim(col_off, first_slice_flag, POSITIONS_LOCAL, 0)
        measured_pattern = lax.dynamic_slice_in_dim(intensity, first_slice_flag, POSITIONS_LOCAL, 0)
        pat_r, pat_i = cut(ext_r, ext_i, rows, cols, width)
        waves_r, waves_i, output_real, output_imaginary = forward_pass(lead_r, lead_i, pat_r, pat_i, kr, ki)
        chirp_real, chirp_imaginary = target_amplitude(output_real, output_imaginary, measured_pattern, wave_real, wave_imaginary)
        chirp_real, chirp_imaginary, term_r, term_i = backward_pass(chirp_real, chirp_imaginary, waves_r, waves_i, pat_r, pat_i, kr, ki)
        return (deposit(acc[0], acc[1], term_r, term_i, rows, cols), None)
    zeros = jnp.zeros((SLICES, OBJ_ROWS + width, OBJ_COLS), jnp.float32)
    (acc_r, acc_i), _ = lax.scan(group, (zeros, zeros), jnp.arange(N_POS, dtype=jnp.int32))
    grad_real = acc_r[:, :OBJ_ROWS].at[:, :width].add(acc_r[:, OBJ_ROWS:])
    grad_imag = acc_i[:, :OBJ_ROWS].at[:, :width].add(acc_i[:, OBJ_ROWS:])
    return (grad_real, grad_imag)
```

```python
import functools
import math

import jax
import jax.numpy as jnp
import numpy as np
from jax import lax
from jax.experimental import pallas as pl
from jax.experimental.pallas import tpu as pltpu
from jax.sharding import PartitionSpec as P

F32 = jnp.float32
BF16 = jnp.bfloat16
SMEM = pl.BlockSpec(memory_space=pltpu.SMEM)
VMEM = pl.BlockSpec(memory_space=pltpu.VMEM)
ANY = pl.BlockSpec(memory_space=pl.ANY)
EDGE = 32
CHUNKS = 2


def halves(x):
    high = x.astype(BF16)
    return high, (x - high.astype(F32)).astype(BF16)


def left_mul(high, low, x):
    xh, xl = halves(x)
    left = jnp.concatenate([high, high, low], 1)
    right = jnp.concatenate([xh, xl, xh], 0)
    return jnp.dot(left, right, preferred_element_type=F32)


def right_mul(x, high, low):
    xh, xl = halves(x)
    left = jnp.concatenate([xh, xl, xh], 1)
    right = jnp.concatenate([high, high, low], 0)
    return jnp.dot(left, right, preferred_element_type=F32)


def fourier_left(n):
    steps = np.arange(n)
    angle = 2.0 * math.pi / n * ((steps[:, None] * steps[None, :]) % n)
    norm = 1.0 / math.sqrt(n)
    wr, wi = np.cos(angle) * norm, -np.sin(angle) * norm
    m = np.block([[wr, -wi], [wi, wr]]).astype(np.float32)
    high = m.astype(jnp.bfloat16)
    return jnp.asarray(high), jnp.asarray((m - high.astype(np.float32)).astype(jnp.bfloat16))


def column_place(col, cols_all, span):
    base = jnp.minimum(col // 128 * 128, cols_all - span)
    return pl.multiple_of(base, 128), col - base


def put(high, low, at, block):
    hi, lo = halves(block)
    high[at] = hi
    low[at] = lo


def fused_kernel(
    obj_r, obj_i, probe, ring, intensity, row_off, col_off, wh, wl,
    mine, theirs, places,
    obj_0, obj_1, patch, outbound, waves, chi, edge_out, edge_in, x_out, x_in, x_own, y_out, y_in,
    prev_row, prev_col,
    k_h, k_l, t_h, t_l, m_h, m_l, g_h, g_l, n_h, n_l, q_h, q_l, edge_m,
    sem_obj, sem_prev_s, sem_prev_r, sem_patch_s, sem_patch_r, sem_edge_s, sem_edge_r,
    sem_x_s, sem_x_r, sem_y_s, sem_y_r, sem_mine, sem_term_s, sem_term_r,
):
    n = probe.shape[-1]
    obj_v = (obj_0, obj_1)
    depth = len(obj_v)
    slices = 2 * depth
    width = n // CHUNKS
    span = n + 128
    p, q = lax.axis_index("pos"), lax.axis_index("slab")
    npos = lax.axis_size("pos")
    nxt, prv, oth = lax.rem(p + 1, npos), lax.rem(p + npos - 1, npos), 1 - q
    to_next, to_prev, to_other = {"pos": nxt}, {"pos": prv}, {"slab": oth}

    def remote(src, dst, send, recv, to):
        return pltpu.make_async_remote_copy(
            src_ref=src, dst_ref=dst, send_sem=send, recv_sem=recv,
            device_id=to, device_id_type=pl.DeviceIdType.MESH,
        )

    blocks = obj_0.shape[1]

    def obj_copies(d):
        return [
            pltpu.make_async_copy(
                src.at[d, :, pl.ds(b * 128, 128)], obj_v[d].at[ri, b], sem_obj.at[ri, d, b]
            )
            for ri, src in enumerate((obj_r, obj_i))
            for b in range(blocks)
        ]

    for d in range(depth):
        for copy in obj_copies(d):
            copy.start()

    barrier = pltpu.get_barrier_semaphore()
    for to in (to_next, to_prev, to_other):
        pl.semaphore_signal(barrier, inc=1, device_id=to, device_id_type=pl.DeviceIdType.MESH)

    def toeplitz(k):
        rows = jnp.broadcast_to(ring[k : k + 1, :], (n, 2 * n))
        return pltpu.roll(rows, 0, 1, stride=1, stride_axis=0)

    kr, ki, tr, ti = (toeplitz(k) for k in range(4))

    def embed(high, low, re, im):
        put(high, low, (slice(0, n), slice(0, n)), re)
        put(high, low, (slice(0, n), slice(n, 2 * n)), -im)
        put(high, low, (slice(n, 2 * n), slice(0, n)), im)
        put(high, low, (slice(n, 2 * n), slice(n, 2 * n)), re)

    embed(k_h, k_l, kr[:, :n], ki[:, :n])
    embed(t_h, t_l, tr[:, :n], -ti[:, :n])

    def edge_matrix(at, re, im):
        top = re + pltpu.roll(-im, EDGE, 1)
        bottom = im + pltpu.roll(re, EDGE, 1)
        both = jnp.concatenate([top, bottom], 0)
        high = both.astype(BF16).astype(F32)
        edge_m[at, :, :128] = (high + pltpu.roll(high, 2 * EDGE, 1)).astype(BF16)
        edge_m[at, :, 128:] = (both - high).astype(BF16)

    for at, re, im in ((0, kr, ki), (2, tr, -ti)):
        edge_matrix(at, re[n - EDGE :, n : n + 128], im[n - EDGE :, n : n + 128])
        edge_matrix(
            at + 1,
            pltpu.roll(re[:EDGE, 2 * n - 128 :], EDGE, 1),
            pltpu.roll(im[:EDGE, 2 * n - 128 :], EDGE, 1),
        )

    pl.semaphore_wait(barrier, 3)
    prev_copies = [
        remote(src, dst, sem_prev_s.at[k], sem_prev_r.at[k], to_next)
        for k, (src, dst) in enumerate(((row_off, prev_row), (col_off, prev_col)))
    ]
    for copy in prev_copies:
        copy.start()

    row_index = lax.broadcasted_iota(jnp.int32, (n, n), 0)

    def cut(dst, d, row, col, role):
        keep = row_index >= row if role == 0 else row_index < row
        first = jnp.minimum(col // 128, blocks - span // 128)
        shift = col - first * 128
        for ri in range(2):
            wide = jnp.concatenate([obj_v[d][ri, first + b] for b in range(span // 128)], 1)
            part = pltpu.roll(wide, lax.rem(span - shift, span), 1)[:, :n]
            dst[ri] = jnp.where(keep, part, 0.0)

    def patch_copy(role, d, owner):
        s = owner * depth + d
        return remote(
            outbound.at[role, d], patch.at[role, s],
            sem_patch_s.at[role, d], sem_patch_r.at[role, d], to_other,
        )

    def cut_role(role, rows, cols):
        for d in range(depth):
            if role == 0:
                for copy in obj_copies(d):
                    copy.wait()
            cut(outbound.at[role, d], d, rows[oth], cols[oth], role)
            patch_copy(role, d, q).start()
        for d in range(depth):
            cut(patch.at[role, q * depth + d], d, rows[q], cols[q], role)

    cut_role(0, row_off, col_off)

    row = row_off[q]
    full = left_mul(wh[...], wl[...], jnp.concatenate([kr[:, :n], ki[:, :n]], 0))
    qr, qi = full[:n], full[n:]
    put(m_h, m_l, slice(0, n), pltpu.roll(qr, row, 1))
    put(m_h, m_l, slice(n, 2 * n), pltpu.roll(qi, row, 1))
    nr, ni = qr.T, qi.T
    put(g_h, g_l, slice(0, n), pltpu.roll(nr, row, 0))
    put(g_h, g_l, slice(n, 2 * n), pltpu.roll(-ni, row, 0))
    for k in range(CHUNKS):
        c = slice(k * width, (k + 1) * width)
        put(n_h, n_l, (k, slice(0, n), slice(0, width)), nr[:, c])
        put(n_h, n_l, (k, slice(0, n), slice(width, 2 * width)), ni[:, c])
        put(n_h, n_l, (k, slice(n, 2 * n), slice(0, width)), -ni[:, c])
        put(n_h, n_l, (k, slice(n, 2 * n), slice(width, 2 * width)), nr[:, c])
        put(q_h, q_l, (k, slice(0, width), slice(0, n)), qr[c])
        put(q_h, q_l, (k, slice(0, width), slice(n, 2 * n)), -qi[c])
        put(q_h, q_l, (k, slice(width, 2 * width), slice(0, n)), qi[c])
        put(q_h, q_l, (k, slice(width, 2 * width), slice(n, 2 * n)), qr[c])

    for copy in prev_copies:
        copy.wait()
    cut_role(1, prev_row, prev_col)
    for k, src in enumerate((row_off, prev_row, col_off, prev_col)):
        places[2 * k] = src[q]
        places[2 * k + 1] = src[oth]

    for role, shift in ((0, row), (1, prev_row[q])):
        for ri in range(2):
            waves[role, 0, ri] = pltpu.roll(probe[ri], shift, 0)

    def edge_copy(step, role):
        return remote(
            edge_out.at[step, role], edge_in.at[step, role],
            sem_edge_s.at[step, role], sem_edge_r.at[step, role], (to_next, to_prev)[role],
        )

    def send_edge(step, role, z):
        at = slice(n - EDGE, n) if role == 0 else slice(0, EDGE)
        for ri in range(2):
            edge_out[step, role, ri] = z[at, ri * n : (ri + 1) * n]
        edge_copy(step, role).start()

    def add_edge(step, role, matrix, dst):
        edge_copy(step, 1 - role).wait_recv()
        x = jnp.concatenate([edge_in[step, 1 - role, 0], edge_in[step, 1 - role, 1]], 0)
        xh, xl = halves(x)
        right = jnp.concatenate([xh, xl, xh, jnp.zeros_like(xh)], 0)
        e = jnp.dot(edge_m[matrix + role], right, preferred_element_type=F32)
        at = slice(n - EDGE, n) if role == 0 else slice(0, EDGE)
        for ri in range(2):
            dst[ri, at] += e[ri * EDGE : (ri + 1) * EDGE]

    def await_patch(role, s):
        @pl.when(lax.div(s, depth) == oth)
        def _():
            patch_copy(role, lax.rem(s, depth), oth).wait_recv()

    def exit_wave(role, s):
        await_patch(role, s)
        pr, pi = waves[role, s, 0], waves[role, s, 1]
        o_r, o_i = patch[role, s, 0], patch[role, s, 1]
        return jnp.concatenate([pr * o_r - pi * o_i, pr * o_i + pi * o_r], 1)

    def stack(z):
        return jnp.concatenate([z[:, :n], z[:, n:]], 0)

    def forward(s, _):
        zs = []
        for role in range(2):
            z = right_mul(exit_wave(role, s), t_h[...], t_l[...])
            send_edge(s, role, z)
            zs.append(z)
        for role in range(2):
            y = left_mul(k_h[...], k_l[...], stack(zs[role]))
            waves[role, s + 1, 0] = y[:n]
            waves[role, s + 1, 1] = y[n:]
        for role in range(2):
            add_edge(s, role, 0, waves.at[role, s + 1])
        return 0

    lax.fori_loop(0, slices - 1, forward, 0)

    def x_copy(k):
        return remote(x_out.at[k], x_in.at[k], sem_x_s.at[k], sem_x_r.at[k], to_prev)

    def y_copy(k):
        return remote(y_out.at[k], y_in.at[k], sem_y_s.at[k], sem_y_r.at[k], to_next)

    last = slices - 1
    u = exit_wave(1, last)
    for k in range(CHUNKS):
        x_out[k] = right_mul(u, n_h[k], n_l[k])
        x_copy(k).start()
    u = exit_wave(0, last)
    for k in range(CHUNKS):
        x_own[k] = right_mul(u, n_h[k], n_l[k])

    def complex_left(high, low, x):
        w = x.shape[1] // 2
        out = left_mul(high, low, x)
        return out[:n, :w] - out[n:, w:], out[:n, w:] + out[n:, :w]

    for k in range(CHUNKS):
        x_copy(k).wait_recv()
        x = jnp.where(row_index >= row, x_own[k], x_in[k])
        fr, fi = complex_left(m_h[...], m_l[...], x)
        residual = 2.0 * (fr * fr + fi * fi - intensity[q, :, k * width : (k + 1) * width])
        g = jnp.concatenate([residual * fr, residual * fi], 1)
        yr, yi = complex_left(g_h[...], g_l[...], g)
        y_out[k] = jnp.concatenate([yr, yi], 1)
        y_copy(k).start()

    def finish(role, s, a_r, a_i):
        w_r, w_i = waves[role, s, 0], waves[role, s, 1]
        o_r, o_i = patch[role, s, 0], patch[role, s, 1]
        chi[role, 0] = a_r * o_r + a_i * o_i
        chi[role, 1] = a_i * o_r - a_r * o_i
        patch[role, s, 0] = a_r * w_r + a_i * w_i
        patch[role, s, 1] = a_i * w_r - a_r * w_i
        d = lax.rem(s, depth)
        own = lax.div(s, depth) == q

        @pl.when(own)
        def _():
            mine_copy(role, d).start()

        @pl.when(jnp.logical_not(own))
        def _():
            term_copy(role, d).start()

    def mine_copy(role, d):
        return pltpu.make_async_copy(
            patch.at[role, q * depth + d], mine.at[role, d], sem_mine.at[role, d]
        )

    def term_copy(role, d):
        return remote(
            patch.at[role, oth * depth + d], theirs.at[role, d],
            sem_term_s.at[role, d], sem_term_r.at[role, d], to_other,
        )

    for role in range(2):
        a = jnp.zeros((n, 2 * n), F32)
        for k in range(CHUNKS):
            if role == 1:
                y_copy(k).wait_recv()
            a += right_mul((y_out, y_in)[role][k], q_h[k], q_l[k])
        finish(role, last, a[:, :n], a[:, n:])

    def backward(i, _):
        s = last - 1 - i
        step = last + i
        zs = []
        for role in range(2):
            z = right_mul(
                jnp.concatenate([chi[role, 0], chi[role, 1]], 1), k_h[...], k_l[...]
            )
            send_edge(step, role, z)
            zs.append(z)
        for role in range(2):
            y = left_mul(t_h[...], t_l[...], stack(zs[role]))
            chi[role, 0] = y[:n]
            chi[role, 1] = y[n:]
        for role in range(2):
            add_edge(step, role, 2, chi.at[role])
            finish(role, s, chi[role, 0], chi[role, 1])
        return 0

    lax.fori_loop(0, slices - 1, backward, 0)

    for copy in [patch_copy(role, d, q) for role in range(2) for d in range(depth)]:
        copy.wait_send()
    for step in range(2 * (slices - 1)):
        for role in range(2):
            edge_copy(step, role).wait_send()
    for k in range(CHUNKS):
        x_copy(k).wait_send()
        y_copy(k).wait_send()
    for role in range(2):
        for d in range(depth):
            mine_copy(role, d).wait()
            term_copy(role, d).wait()


def deposit_kernel(places, mine, theirs, out_r, out_i):
    n = mine.shape[-1]
    span = n + 128
    row_index = lax.broadcasted_iota(jnp.int32, (n, n), 0)
    for ri, out in enumerate((out_r, out_i)):
        out[...] = jnp.zeros_like(out)
        for k in range(4):
            role, src = k // 2, (mine, theirs)[k % 2]
            row, col = places[k], places[4 + k]
            keep = row_index >= row if role == 0 else row_index < row
            term = jnp.where(keep, src[role, 0, ri], 0.0)
            base, shift = column_place(col, out.shape[-1], span)
            wide = jnp.concatenate([term, jnp.zeros((n, 128), F32)], 1)
            out[0, :, pl.ds(base, span)] += pltpu.roll(wide, shift, 1)


def local(obj_real, obj_imag, probe, taps, intensity, row_off, col_off):
    n = probe.shape[-1]
    depth, tile, cols_all = obj_real.shape
    slices = 2 * depth
    half = (taps.shape[1] - 1) // 2
    gap = jnp.zeros((2, 2 * n - taps.shape[1]), F32)
    back = taps[:, ::-1]
    ring = jnp.concatenate(
        [jnp.concatenate([t[:, half:], gap, t[:, :half]], 1) for t in (taps, back)], 0
    )
    wide = 2 * n // CHUNKS
    steps = 2 * (slices - 1)
    dma = pltpu.SemaphoreType.DMA
    square = pltpu.VMEM((2 * n, 2 * n), BF16)
    terms = jax.ShapeDtypeStruct((2, depth, 2, n, n), F32)
    mine, theirs, places = pl.pallas_call(
        fused_kernel,
        out_shape=[terms, terms, jax.ShapeDtypeStruct((8,), jnp.int32)],
        in_specs=[ANY, ANY, VMEM, VMEM, VMEM, SMEM, SMEM, VMEM, VMEM],
        out_specs=[ANY, ANY, SMEM],
        scratch_shapes=[
            pltpu.VMEM((2, cols_all // 128, tile, 128), F32),
            pltpu.VMEM((2, cols_all // 128, tile, 128), F32),
            pltpu.VMEM((2, slices, 2, n, n), F32),
            pltpu.VMEM((2, depth, 2, n, n), F32),
            pltpu.VMEM((2, slices, 2, n, n), F32),
            pltpu.VMEM((2, 2, n, n), F32),
            pltpu.VMEM((steps, 2, 2, EDGE, n), F32),
            pltpu.VMEM((steps, 2, 2, EDGE, n), F32),
        ]
        + [pltpu.VMEM((CHUNKS, n, wide), F32)] * 5
        + [pltpu.SMEM((2,), jnp.int32)] * 2
        + [square] * 4
        + [pltpu.VMEM((2 * n, n), BF16)] * 4
        + [pltpu.VMEM((CHUNKS, 2 * n, wide), BF16)] * 2
        + [pltpu.VMEM((CHUNKS, wide, 2 * n), BF16)] * 2
        + [pltpu.VMEM((4, 2 * EDGE, 256), BF16)]
        + [
            dma((2, depth, cols_all // 128)), dma((2,)), dma((2,)),
            dma((2, depth)), dma((2, depth)),
            dma((steps, 2)), dma((steps, 2)),
            dma((CHUNKS,)), dma((CHUNKS,)), dma((CHUNKS,)), dma((CHUNKS,)),
            dma((2, depth)), dma((2, depth)), dma((2, depth)),
        ],
        compiler_params=pltpu.CompilerParams(
            collective_id=0, has_side_effects=True, vmem_limit_bytes=56 * 2**20
        ),
        name="fused",
    )(obj_real, obj_imag, probe, ring, intensity, row_off, col_off, *fourier_left(n))

    terms_spec = pl.BlockSpec((2, 1, 2, n, n), lambda d: (0, d, 0, 0, 0))
    plane_spec = pl.BlockSpec((1, tile, cols_all), lambda d: (d, 0, 0))
    return pl.pallas_call(
        deposit_kernel,
        grid=(depth,),
        out_shape=[jax.ShapeDtypeStruct(obj_real.shape, F32)] * 2,
        in_specs=[SMEM, terms_spec, terms_spec],
        out_specs=[plane_spec] * 2,
        compiler_params=pltpu.CompilerParams(vmem_limit_bytes=40 * 2**20),
        name="deposit",
    )(places, mine, theirs)


def solution(mesh):
    in_specs = (
        P(("parts", "slab"), "pos", None),
        P(("parts", "slab"), "pos", None),
        P(),
        P(),
        P(("parts", "pos"), None, None),
        P(("parts", "pos")),
        P(("parts", "pos")),
    )
    out_specs = (P(("parts", "slab"), "pos", None), P(("parts", "slab"), "pos", None))
    return jax.shard_map(local, mesh=mesh, in_specs=in_specs, out_specs=out_specs, check_vma=False)
```

```python
import functools
import math

import jax
import jax.numpy as jnp
import numpy as np
from jax import lax
from jax.experimental import pallas as pl
from jax.experimental.pallas import tpu as pltpu
from jax.sharding import PartitionSpec as P

F32 = jnp.float32
BF16 = jnp.bfloat16
SMEM = pl.BlockSpec(memory_space=pltpu.SMEM)
VMEM = pl.BlockSpec(memory_space=pltpu.VMEM)
ANY = pl.BlockSpec(memory_space=pl.ANY)
CHUNKS = 2
EDGE = 32


def halves(x):
    high = x.astype(BF16)
    return high, (x - high.astype(F32)).astype(BF16)


def left_mul(high, low, x):
    xh, xl = halves(x)
    left = jnp.concatenate([high, high, low], 1)
    right = jnp.concatenate([xh, xl, xh], 0)
    return jnp.dot(left, right, preferred_element_type=F32)


def right_mul(x, high, low):
    xh, xl = halves(x)
    left = jnp.concatenate([xh, xl, xh], 1)
    right = jnp.concatenate([high, high, low], 0)
    return jnp.dot(left, right, preferred_element_type=F32)


def fourier_left(n):
    steps = np.arange(n)
    angle = 2.0 * math.pi / n * ((steps[:, None] * steps[None, :]) % n)
    norm = 1.0 / math.sqrt(n)
    m = np.concatenate([np.cos(angle) * norm, -np.sin(angle) * norm], 0).astype(np.float32)
    high = m.astype(jnp.bfloat16)
    return jnp.asarray(high), jnp.asarray((m - high.astype(np.float32)).astype(jnp.bfloat16))


def put(high, low, at, block):
    hi, lo = halves(block)
    high[at] = hi
    low[at] = lo


def embed(high, low, re, im):
    n = re.shape[0]
    one, two = slice(0, n), slice(n, 2 * n)
    for ref, r, i in zip((high, low), halves(re), halves(im)):
        ref[one, one] = r
        ref[one, two] = -i
        ref[two, one] = i
        ref[two, two] = r


def strip_rows(slices, half):
    forward = [half * (slices - 1 - s) for s in range(slices)]
    backward = [half * s for s in range(slices)]
    return [[-(-rows // 8) * 8 for rows in need] for need in (forward, backward)]


def fused_kernel(
    obj_r, obj_i, probe_any, taps, intensity_any, row_off, col_off, wh_any, wl_any,
    mine, theirs, places,
    obj_0, obj_1, probe, intensity, wh, wl, patch, outbound, strips, waves, chi, terms,
    x_out, x_in, x_own, y_out, y_in, ring, prev_row, prev_col,
    k_h, k_l, t_h, t_l, kb_h, kb_l, tt_h, tt_l,
    m_h, m_l, g_h, g_l, n_h, n_l, q_h, q_l, edge_out, edge_in, edge_m,
    sem_obj, sem_in, sem_prev_s, sem_prev_r, sem_patch_s, sem_patch_r, sem_strip_s, sem_strip_r,
    sem_edge_s, sem_edge_r, sem_x_s, sem_x_r, sem_y_s, sem_y_r, sem_mine, sem_term_s, sem_term_r,
):
    n = probe.shape[-1]
    obj_v = (obj_0, obj_1)
    depth = len(obj_v)
    slices = 2 * depth
    last = slices - 1
    width = n // CHUNKS
    span = n + 128
    taps_count = taps.shape[1]
    half = (taps_count - 1) // 2
    extent = strip_rows(slices, half)
    p, q = lax.axis_index("pos"), lax.axis_index("slab")
    npos = lax.axis_size("pos")
    nxt, prv, oth = lax.rem(p + 1, npos), lax.rem(p + npos - 1, npos), 1 - q

    def remote(src, dst, send, recv, pos, slab):
        return pltpu.make_async_remote_copy(
            src_ref=src, dst_ref=dst, send_sem=send, recv_sem=recv,
            device_id={"pos": pos, "slab": slab}, device_id_type=pl.DeviceIdType.MESH,
        )

    blocks = obj_0.shape[1]

    def obj_copies(d):
        return [
            pltpu.make_async_copy(
                src.at[d, :, pl.ds(b * 128, 128)], obj_v[d].at[ri, b], sem_obj.at[ri, d, b]
            )
            for ri, src in enumerate((obj_r, obj_i))
            for b in range(blocks)
        ]

    for d in range(depth):
        for copy in obj_copies(d):
            copy.start()
    small = [
        pltpu.make_async_copy(src, dst, sem_in.at[k])
        for k, (src, dst) in enumerate(
            ((wh_any, wh), (wl_any, wl), (probe_any, probe), (intensity_any.at[q], intensity))
        )
    ]
    for copy in small:
        copy.start()

    barrier = pltpu.get_barrier_semaphore()
    for pos, slab in ((nxt, q), (nxt, oth), (prv, q), (prv, oth), (p, oth)):
        pl.semaphore_signal(
            barrier, inc=1, device_id={"pos": pos, "slab": slab},
            device_id_type=pl.DeviceIdType.MESH,
        )

    row_index = lax.broadcasted_iota(jnp.int32, (n, n), 0)
    col_index = lax.broadcasted_iota(jnp.int32, (n, n), 1)
    near = jnp.abs(row_index - col_index) < n // 2

    def cut(dst, d, row, col, role):
        keep = row_index >= row if role == 0 else row_index < row
        first = jnp.minimum(col // 128, blocks - span // 128)
        shift = col - first * 128
        for ri in range(2):
            wide = jnp.concatenate([obj_v[d][ri, first + b] for b in range(span // 128)], 1)
            part = pltpu.roll(wide, lax.rem(span - shift, span), 1)[:, :n]
            dst[ri] = jnp.where(keep, part, 0.0)

    def patch_copy(role, d, owner):
        return remote(
            outbound.at[role, d], patch.at[role, owner * depth + d],
            sem_patch_s.at[role, d], sem_patch_r.at[role, d], p, oth,
        )

    def strip_copy(role, s, slab):
        rows = extent[role][s]
        at = pl.ds(n - rows, rows) if role == 0 else pl.ds(0, rows)
        src = patch.at[role, s, :, at] if slab == 0 else outbound.at[role, s % depth, :, at]
        return remote(
            src, strips.at[1 - role, s, :, pl.ds(0, rows)],
            sem_strip_s.at[role, s, slab], sem_strip_r.at[1 - role, s],
            (nxt, prv)[role], (q, oth)[slab],
        )

    group = (tuple(range(last)), tuple(range(last, 0, -1)))

    def send_strips(role):
        for s in group[role]:
            @pl.when(q == s // depth)
            def _():
                for slab in range(2):
                    strip_copy(role, s, slab).start()

    def cut_role(role, rows, cols):
        for d in range(depth):
            if role == 0:
                for copy in obj_copies(d):
                    copy.wait()
            cut(outbound.at[role, d], d, rows[oth], cols[oth], role)
            cut(patch.at[role, q * depth + d], d, rows[q], cols[q], role)

    def send_role(role):
        for d in range(depth):
            patch_copy(role, d, q).start()

    cut_role(0, row_off, col_off)
    pl.semaphore_wait(barrier, 5)
    prev_copies = [
        remote(src, dst, sem_prev_s.at[k], sem_prev_r.at[k], nxt, q)
        for k, (src, dst) in enumerate(((row_off, prev_row), (col_off, prev_col)))
    ]
    for copy in prev_copies:
        copy.start()
    send_strips(0)
    send_role(0)

    ring[...] = jnp.zeros_like(ring)
    ring[:2, :taps_count] = taps[...]
    tap = pltpu.roll(ring[...], n - half, 1)

    def circulant(k):
        rows = jnp.broadcast_to(tap[k : k + 1, :], (n, n))
        return pltpu.roll(rows, 0, 1, stride=1, stride_axis=0)

    cr, ci = circulant(0), circulant(1)
    er, ei = cr.T, -ci.T

    def masked(keep, re, im):
        return jnp.where(keep, re, 0.0), jnp.where(keep, im, 0.0)

    def cut_mask(row):
        return ((row_index < row) == (col_index < row)) == near

    def edge_matrix(at, re, im):
        top = re + pltpu.roll(-im, EDGE, 1)
        bottom = im + pltpu.roll(re, EDGE, 1)
        both = jnp.concatenate([top, bottom], 0)
        high = both.astype(BF16).astype(F32)
        edge_m[at, :, :128] = (high + pltpu.roll(high, 2 * EDGE, 1)).astype(BF16)
        edge_m[at, :, 128:] = (both - high).astype(BF16)

    def edge_copy(way, step):
        return remote(
            edge_out.at[way, step], edge_in.at[way, step],
            sem_edge_s.at[way, step], sem_edge_r.at[way, step], (prv, nxt)[way], q,
        )

    def send_edge(way, step, z):
        at = slice(0, EDGE) if way == 0 else slice(n - EDGE, n)
        for ri in range(2):
            edge_out[way, step, ri] = z[at, ri * n : (ri + 1) * n]
        edge_copy(way, step).start()

    def edge_term(way, step):
        edge_copy(way, step).wait_recv()
        xh, xl = halves(jnp.concatenate([edge_in[way, step, 0], edge_in[way, step, 1]], 0))
        right = jnp.concatenate([xh, xl, xh, jnp.zeros_like(xh)], 0)
        return jnp.dot(edge_m[way], right, preferred_element_type=F32)

    def await_patch(role, s):
        @pl.when(q != s // depth)
        def _():
            patch_copy(role, s % depth, oth).wait_recv()

    def add_strip(role, s):
        rows = extent[1 - role][s]
        at = slice(0, rows) if role == 0 else slice(n - rows, n)
        strip_copy(1 - role, s, 0).wait_recv()
        for ri in range(2):
            patch[role, s, ri, at] += strips[role, s, ri, :rows]

    def exit_wave(role, s):
        pr, pi = waves[role, s, 0], waves[role, s, 1]
        o_r, o_i = patch[role, s, 0], patch[role, s, 1]
        return jnp.concatenate([pr * o_r - pi * o_i, pr * o_i + pi * o_r], 1)

    def stack(z):
        return jnp.concatenate([z[:, :n], z[:, n:]], 0)

    def step_top(s):
        await_patch(0, s)
        z = right_mul(exit_wave(0, s), t_h[...], t_l[...])
        y = left_mul(k_h[...], k_l[...], stack(z))
        waves[0, s + 1, 0] = y[:n]
        waves[0, s + 1, 1] = y[n:]

    def edge_top(s):
        e = edge_term(0, s)
        for ri in range(2):
            waves[0, s + 1, ri, n - EDGE :] += e[ri * EDGE : (ri + 1) * EDGE]

    def step_bottom(s):
        await_patch(1, s)
        add_strip(1, s)
        z = right_mul(exit_wave(1, s), t_h[...], t_l[...])
        send_edge(0, s, z)
        y = left_mul(kb_h[...], kb_l[...], stack(z))
        waves[1, s + 1, 0] = y[:n]
        waves[1, s + 1, 1] = y[n:]

    row = row_off[q]
    kr, ki = masked(near, cr, ci)
    embed(t_h, t_l, *masked(near, er, ei))
    embed(k_h, k_l, kr, ki)
    edge_matrix(0, cr[n - EDGE :, :128], ci[n - EDGE :, :128])
    edge_matrix(
        1, pltpu.roll(er[:EDGE, n - 128 :], EDGE, 1), pltpu.roll(ei[:EDGE, n - 128 :], EDGE, 1)
    )
    for copy in small:
        copy.wait()
    for ri in range(2):
        waves[0, 0, ri] = pltpu.roll(probe[ri], row, 0)
    step_top(0)

    for copy in prev_copies:
        copy.wait()
    cut_role(1, prev_row, prev_col)
    send_role(1)
    for k, src in enumerate((row_off, prev_row, col_off, prev_col)):
        places[2 * k] = src[q]
        places[2 * k + 1] = src[oth]

    back = prev_row[q]
    embed(kb_h, kb_l, *masked(cut_mask(back), cr, ci))
    for ri in range(2):
        waves[1, 0, ri] = pltpu.roll(probe[ri], back, 0)

    def complex_left(high, low, x):
        w = x.shape[1] // 2
        out = left_mul(high, low, x)
        return out[:n, :w] - out[n:, w:], out[:n, w:] + out[n:, :w]

    qr, qi = complex_left(wh[...], wl[...], jnp.concatenate([kr, ki], 1))
    nr, ni = qr.T, qi.T
    for k in range(CHUNKS):
        c = slice(k * width, (k + 1) * width)
        put(n_h, n_l, (k, slice(0, n), slice(0, width)), nr[:, c])
        put(n_h, n_l, (k, slice(0, n), slice(width, 2 * width)), ni[:, c])
        put(n_h, n_l, (k, slice(n, 2 * n), slice(0, width)), -ni[:, c])
        put(n_h, n_l, (k, slice(n, 2 * n), slice(width, 2 * width)), nr[:, c])
        put(q_h, q_l, (k, slice(0, width), slice(0, n)), qr[c])
        put(q_h, q_l, (k, slice(0, width), slice(n, 2 * n)), -qi[c])
        put(q_h, q_l, (k, slice(width, 2 * width), slice(0, n)), qi[c])
        put(q_h, q_l, (k, slice(width, 2 * width), slice(n, 2 * n)), qr[c])

    def x_copy(k):
        return remote(x_out.at[k], x_in.at[k], sem_x_s.at[k], sem_x_r.at[k], prv, q)

    def y_copy(k):
        return remote(y_out.at[k], y_in.at[k], sem_y_s.at[k], sem_y_r.at[k], nxt, q)

    step_bottom(0)
    for s in range(1, last):
        step_bottom(s)
    await_patch(1, last)
    u = exit_wave(1, last)
    for k in range(CHUNKS):
        x_out[k] = right_mul(u, n_h[k], n_l[k])
        x_copy(k).start()
    send_strips(1)

    for s in range(1, last):
        edge_top(s - 1)
        step_top(s)
    put(m_h, m_l, slice(0, n), pltpu.roll(qr, row, 1))
    put(m_h, m_l, slice(n, 2 * n), pltpu.roll(qi, row, 1))
    put(g_h, g_l, slice(0, n), pltpu.roll(nr, row, 0))
    put(g_h, g_l, slice(n, 2 * n), pltpu.roll(-ni, row, 0))
    embed(tt_h, tt_l, *masked(cut_mask(row), er, ei))
    edge_top(last - 1)
    await_patch(0, last)
    u = exit_wave(0, last)
    for k in range(CHUNKS):
        x_own[k] = right_mul(u, n_h[k], n_l[k])

    for k in range(CHUNKS):
        x_copy(k).wait_recv()
        x = jnp.where(row_index >= row, x_own[k], x_in[k])
        fr, fi = complex_left(m_h[...], m_l[...], x)
        residual = 2.0 * (fr * fr + fi * fi - intensity[:, k * width : (k + 1) * width])
        g = jnp.concatenate([residual * fr, residual * fi], 1)
        yr, yi = complex_left(g_h[...], g_l[...], g)
        y_out[k] = jnp.concatenate([yr, yi], 1)
        y_copy(k).start()

    def mine_copy(role, d):
        return pltpu.make_async_copy(
            terms.at[role, q * depth + d], mine.at[role, d], sem_mine.at[role, d]
        )

    def term_copy(role, d):
        return remote(
            terms.at[role, oth * depth + d], theirs.at[role, d],
            sem_term_s.at[role, d], sem_term_r.at[role, d], p, oth,
        )

    def finish(role, s, a_r, a_i):
        w_r, w_i = waves[role, s, 0], waves[role, s, 1]
        terms[role, s, 0] = a_r * w_r + a_i * w_i
        terms[role, s, 1] = a_i * w_r - a_r * w_i
        if s > 0:
            o_r, o_i = patch[role, s, 0], patch[role, s, 1]
            if role == 1:
                o_r, o_i = masked(row_index < back, o_r, o_i)
            chi[role, 0] = a_r * o_r + a_i * o_i
            chi[role, 1] = a_i * o_r - a_r * o_i

        @pl.when(q == s // depth)
        def _():
            mine_copy(role, s % depth).start()

        @pl.when(q != s // depth)
        def _():
            term_copy(role, s % depth).start()

    for role in range(2):
        if role == 0:
            add_strip(0, last)
        a = jnp.zeros((n, 2 * n), F32)
        for k in range(CHUNKS):
            if role == 1:
                y_copy(k).wait_recv()
            a += right_mul((y_out, y_in)[role][k], q_h[k], q_l[k])
        finish(role, last, a[:, :n], a[:, n:])
        for s in range(last - 1, -1, -1):
            z = right_mul(
                jnp.concatenate([chi[role, 0], chi[role, 1]], 1), k_h[...], k_l[...]
            )
            if role == 0:
                send_edge(1, s, z)
                y = left_mul(tt_h[...], tt_l[...], stack(z))
                if s > 0:
                    add_strip(0, s)
            else:
                y = left_mul(t_h[...], t_l[...], stack(z))
                e = edge_term(1, s)
                y = jnp.concatenate(
                    [y[:EDGE] + e[:EDGE], y[EDGE:n], y[n : n + EDGE] + e[EDGE:], y[n + EDGE :]], 0
                )
            finish(role, s, y[:n], y[n:])

    for role in range(2):
        for d in range(depth):
            patch_copy(role, d, q).wait_send()
        for s in group[role]:
            @pl.when(q == s // depth)
            def _():
                for slab in range(2):
                    strip_copy(role, s, slab).wait_send()
        for s in range(last):
            edge_copy(role, s).wait_send()
    for k in range(CHUNKS):
        x_copy(k).wait_send()
        y_copy(k).wait_send()
    for role in range(2):
        for d in range(depth):
            mine_copy(role, d).wait()
            term_copy(role, d).wait()


def column_place(col, cols_all, span):
    base = jnp.minimum(col // 128 * 128, cols_all - span)
    return pl.multiple_of(base, 128), col - base


def deposit_kernel(places, mine, theirs, out_r, out_i):
    n = mine.shape[-1]
    span = n + 128
    row_index = lax.broadcasted_iota(jnp.int32, (n, n), 0)
    for ri, out in enumerate((out_r, out_i)):
        out[...] = jnp.zeros_like(out)
        for k in range(4):
            role, src = k // 2, (mine, theirs)[k % 2]
            row, col = places[k], places[4 + k]
            keep = row_index >= row if role == 0 else row_index < row
            term = jnp.where(keep, src[role, 0, ri], 0.0)
            base, shift = column_place(col, out.shape[-1], span)
            wide = jnp.concatenate([term, jnp.zeros((n, 128), F32)], 1)
            out[0, :, pl.ds(base, span)] += pltpu.roll(wide, shift, 1)


def local(obj_real, obj_imag, probe, taps, intensity, row_off, col_off):
    n = probe.shape[-1]
    depth, tile, cols_all = obj_real.shape
    slices = 2 * depth
    wide = 2 * n // CHUNKS
    longest = max(max(strip_rows(slices, (taps.shape[1] - 1) // 2)))
    dma = pltpu.SemaphoreType.DMA
    terms = jax.ShapeDtypeStruct((2, depth, 2, n, n), F32)
    half_obj = pltpu.VMEM((2, cols_all // 128, tile, 128), F32)
    windows = pltpu.VMEM((2, slices, 2, n, n), F32)
    mine, theirs, places = pl.pallas_call(
        fused_kernel,
        out_shape=[terms, terms, jax.ShapeDtypeStruct((8,), jnp.int32)],
        in_specs=[ANY, ANY, ANY, VMEM, ANY, SMEM, SMEM, ANY, ANY],
        out_specs=[ANY, ANY, SMEM],
        scratch_shapes=[
            half_obj, half_obj,
            pltpu.VMEM((2, n, n), F32),
            pltpu.VMEM((n, n), F32),
            pltpu.VMEM((2 * n, n), BF16),
            pltpu.VMEM((2 * n, n), BF16),
            windows,
            pltpu.VMEM((2, depth, 2, n, n), F32),
            pltpu.VMEM((2, slices, 2, longest, n), F32),
            windows,
            pltpu.VMEM((2, 2, n, n), F32),
            windows,
        ]
        + [pltpu.VMEM((CHUNKS, n, wide), F32)] * 5
        + [pltpu.VMEM((8, n), F32)]
        + [pltpu.SMEM((2,), jnp.int32)] * 2
        + [pltpu.VMEM((2 * n, 2 * n), BF16)] * 8
        + [pltpu.VMEM((2 * n, n), BF16)] * 4
        + [pltpu.VMEM((CHUNKS, 2 * n, wide), BF16)] * 2
        + [pltpu.VMEM((CHUNKS, wide, 2 * n), BF16)] * 2
        + [pltpu.VMEM((2, slices - 1, 2, EDGE, n), F32)] * 2
        + [pltpu.VMEM((2, 2 * EDGE, 8 * EDGE), BF16)]
        + [
            dma((2, depth, cols_all // 128)), dma((4,)), dma((2,)), dma((2,)),
            dma((2, depth)), dma((2, depth)), dma((2, slices, 2)), dma((2, slices)),
            dma((2, slices - 1)), dma((2, slices - 1)),
            dma((CHUNKS,)), dma((CHUNKS,)), dma((CHUNKS,)), dma((CHUNKS,)),
            dma((2, depth)), dma((2, depth)), dma((2, depth)),
        ],
        compiler_params=pltpu.CompilerParams(
            collective_id=0, has_side_effects=True, vmem_limit_bytes=60 * 2**20
        ),
        name="fused",
    )(obj_real, obj_imag, probe, taps, intensity, row_off, col_off, *fourier_left(n))

    terms_spec = pl.BlockSpec((2, 1, 2, n, n), lambda d: (0, d, 0, 0, 0))
    plane_spec = pl.BlockSpec((1, tile, cols_all), lambda d: (d, 0, 0))
    return pl.pallas_call(
        deposit_kernel,
        grid=(depth,),
        out_shape=[jax.ShapeDtypeStruct(obj_real.shape, F32)] * 2,
        in_specs=[SMEM, terms_spec, terms_spec],
        out_specs=[plane_spec] * 2,
        compiler_params=pltpu.CompilerParams(vmem_limit_bytes=60 * 2**20),
        name="deposit",
    )(places, mine, theirs)


def solution(mesh):
    in_specs = (
        P(("parts", "slab"), "pos", None),
        P(("parts", "slab"), "pos", None),
        P(),
        P(),
        P(("parts", "pos"), None, None),
        P(("parts", "pos")),
        P(("parts", "pos")),
    )
    out_specs = (P(("parts", "slab"), "pos", None), P(("parts", "slab"), "pos", None))
    return jax.shard_map(local, mesh=mesh, in_specs=in_specs, out_specs=out_specs, check_vma=False)
```

```python
import functools
import math

import jax
import jax.numpy as jnp
import numpy as np
from jax import lax
from jax.experimental import pallas as pl
from jax.experimental.pallas import tpu as pltpu
from jax.sharding import PartitionSpec as P

F32 = jnp.float32
BF16 = jnp.bfloat16
SMEM = pl.BlockSpec(memory_space=pltpu.SMEM)
VMEM = pl.BlockSpec(memory_space=pltpu.VMEM)
ANY = pl.BlockSpec(memory_space=pl.ANY)
CHUNKS = 2
EDGE = 32
PIECES = 2


def halves(x):
    high = x.astype(BF16)
    return high, (x - high.astype(F32)).astype(BF16)


def left_mul(high, low, x):
    xh, xl = halves(x)
    left = jnp.concatenate([high, high, low], 1)
    right = jnp.concatenate([xh, xl, xh], 0)
    return jnp.dot(left, right, preferred_element_type=F32)


def right_mul(x, high, low):
    xh, xl = halves(x)
    left = jnp.concatenate([xh, xl, xh], 1)
    right = jnp.concatenate([high, high, low], 0)
    return jnp.dot(left, right, preferred_element_type=F32)


def fourier_left(n):
    steps = np.arange(n)
    angle = 2.0 * math.pi / n * ((steps[:, None] * steps[None, :]) % n)
    norm = 1.0 / math.sqrt(n)
    m = np.concatenate([np.cos(angle) * norm, -np.sin(angle) * norm], 0).astype(np.float32)
    high = m.astype(jnp.bfloat16)
    return jnp.asarray(high), jnp.asarray((m - high.astype(np.float32)).astype(jnp.bfloat16))


def put(high, low, at, block):
    hi, lo = halves(block)
    high[at] = hi
    low[at] = lo


def embed(high, low, re, im):
    n = re.shape[0]
    one, two = slice(0, n), slice(n, 2 * n)
    for ref, r, i in zip((high, low), halves(re), halves(im)):
        ref[one, one] = r
        ref[one, two] = -i
        ref[two, one] = i
        ref[two, two] = r


def strip_rows(slices, half):
    forward = [half * (slices - 1 - s) for s in range(slices)]
    backward = [half * s for s in range(slices)]
    return [[-(-rows // 8) * 8 for rows in need] for need in (forward, backward)]


def fused_kernel(
    obj_r, obj_i, probe_any, taps, intensity_any, row_off, col_off, wh_any, wl_any,
    mine, theirs, places,
    obj_0, obj_1, probe, intensity, wh, wl, patch, outbound, strips, waves, chi, terms,
    x_out, x_in, x_own, y_out, y_in, ring, prev_row, prev_col,
    k_h, k_l, t_h, t_l, kb_h, kb_l, tt_h, tt_l,
    m_h, m_l, g_h, g_l, n_h, n_l, q_h, q_l, edge_out, edge_in, edge_m,
    sem_obj, sem_in, sem_prev_s, sem_prev_r, sem_patch_s, sem_patch_r, sem_strip_s, sem_strip_r,
    sem_edge_s, sem_edge_r, sem_x_s, sem_x_r, sem_y_s, sem_y_r, sem_mine, sem_term_s, sem_term_r,
):
    n = probe.shape[-1]
    obj_v = (obj_0, obj_1)
    depth = len(obj_v)
    slices = 2 * depth
    last = slices - 1
    width = n // CHUNKS
    span = n + 128
    taps_count = taps.shape[1]
    half = (taps_count - 1) // 2
    extent = strip_rows(slices, half)
    p, q = lax.axis_index("pos"), lax.axis_index("slab")
    npos = lax.axis_size("pos")
    nxt, prv, oth = lax.rem(p + 1, npos), lax.rem(p + npos - 1, npos), 1 - q

    def remote(src, dst, send, recv, pos, slab):
        return pltpu.make_async_remote_copy(
            src_ref=src, dst_ref=dst, send_sem=send, recv_sem=recv,
            device_id={"pos": pos, "slab": slab}, device_id_type=pl.DeviceIdType.MESH,
        )

    blocks = obj_0.shape[1]

    def obj_copies(d):
        return [
            pltpu.make_async_copy(
                src.at[d, :, pl.ds(b * 128, 128)], obj_v[d].at[ri, b], sem_obj.at[ri, d, b]
            )
            for ri, src in enumerate((obj_r, obj_i))
            for b in range(blocks)
        ]

    for d in range(depth):
        for copy in obj_copies(d):
            copy.start()
    small = [
        pltpu.make_async_copy(src, dst, sem_in.at[k])
        for k, (src, dst) in enumerate(
            ((wh_any, wh), (wl_any, wl), (probe_any, probe), (intensity_any.at[q], intensity))
        )
    ]
    for copy in small:
        copy.start()

    barrier = pltpu.get_barrier_semaphore()
    for pos, slab in ((nxt, q), (prv, q), (p, oth)):
        pl.semaphore_signal(
            barrier, inc=1, device_id={"pos": pos, "slab": slab},
            device_id_type=pl.DeviceIdType.MESH,
        )

    row_index = lax.broadcasted_iota(jnp.int32, (n, n), 0)
    col_index = lax.broadcasted_iota(jnp.int32, (n, n), 1)
    near = jnp.abs(row_index - col_index) < n // 2
    lane_index = lax.broadcasted_iota(jnp.int32, (n, 128), 1)

    def cut(dst, d, row, col, role):
        keep = row_index >= row if role == 0 else row_index < row
        first = jnp.minimum(col // 128, blocks - span // 128)
        shift = col - first * 128
        left = lane_index < 128 - shift
        for ri in range(2):
            turned = [
                pltpu.roll(obj_v[d][ri, first + b], lax.rem(128 - shift, 128), 1)
                for b in range(span // 128)
            ]
            part = jnp.concatenate(
                [jnp.where(left, a, b) for a, b in zip(turned[:-1], turned[1:])], 1
            )
            dst[ri] = jnp.where(keep, part, 0.0)

    def patch_copy(role, d, owner):
        return remote(
            outbound.at[role, d], patch.at[role, owner * depth + d],
            sem_patch_s.at[role, d], sem_patch_r.at[role, d], p, oth,
        )

    def strip_copy(role, s):
        rows = extent[role][s]
        at = pl.ds(n - rows, rows) if role == 0 else pl.ds(0, rows)
        return remote(
            patch.at[role, s, :, at], strips.at[1 - role, s, :, pl.ds(0, rows)],
            sem_strip_s.at[role, s], sem_strip_r.at[1 - role, s], (nxt, prv)[role], q,
        )

    def await_patch(role, s):
        @pl.when(q != s // depth)
        def _():
            patch_copy(role, s % depth, oth).wait_recv()

    group = (tuple(range(last)), tuple(range(last, 0, -1)))

    def cut_role(role, rows, cols):
        for d in range(depth):
            if role == 0:
                for copy in obj_copies(d):
                    copy.wait()
            cut(outbound.at[role, d], d, rows[oth], cols[oth], role)
            cut(patch.at[role, q * depth + d], d, rows[q], cols[q], role)

    def send_role(role):
        for d in range(depth):
            patch_copy(role, d, q).start()

    cut_role(0, row_off, col_off)
    pl.semaphore_wait(barrier, 3)
    prev_copies = [
        remote(src, dst, sem_prev_s.at[k], sem_prev_r.at[k], nxt, q)
        for k, (src, dst) in enumerate(((row_off, prev_row), (col_off, prev_col)))
    ]
    for copy in prev_copies:
        copy.start()
    send_role(0)
    for s in group[0]:
        await_patch(0, s)
        strip_copy(0, s).start()

    ring[...] = jnp.zeros_like(ring)
    ring[:2, :taps_count] = taps[...]
    tap = pltpu.roll(ring[...], n - half, 1)

    def circulant(k):
        rows = jnp.broadcast_to(tap[k : k + 1, :], (n, n))
        return pltpu.roll(rows, 0, 1, stride=1, stride_axis=0)

    cr, ci = circulant(0), circulant(1)
    er, ei = cr.T, -ci.T

    def masked(keep, re, im):
        return jnp.where(keep, re, 0.0), jnp.where(keep, im, 0.0)

    def cut_mask(row):
        return ((row_index < row) == (col_index < row)) == near

    def edge_matrix(at, re, im):
        top = re + pltpu.roll(-im, EDGE, 1)
        bottom = im + pltpu.roll(re, EDGE, 1)
        both = jnp.concatenate([top, bottom], 0)
        high = both.astype(BF16).astype(F32)
        edge_m[at, :, :128] = (high + pltpu.roll(high, 2 * EDGE, 1)).astype(BF16)
        edge_m[at, :, 128:] = (both - high).astype(BF16)

    def edge_copy(way, step):
        return remote(
            edge_out.at[way, step], edge_in.at[way, step],
            sem_edge_s.at[way, step], sem_edge_r.at[way, step], (prv, nxt)[way], q,
        )

    def send_edge(way, step, z):
        at = slice(0, EDGE) if way == 0 else slice(n - EDGE, n)
        for ri in range(2):
            edge_out[way, step, ri] = z[at, ri * n : (ri + 1) * n]
        edge_copy(way, step).start()

    def edge_term(way, step):
        edge_copy(way, step).wait_recv()
        xh, xl = halves(jnp.concatenate([edge_in[way, step, 0], edge_in[way, step, 1]], 0))
        right = jnp.concatenate([xh, xl, xh, jnp.zeros_like(xh)], 0)
        return jnp.dot(edge_m[way], right, preferred_element_type=F32)

    def add_strip(role, s):
        rows = extent[1 - role][s]
        strip_copy(1 - role, s).wait_recv()
        for ri in range(2):
            patch[role, s, ri, n - rows :] += strips[role, s, ri, :rows]

    def exit_wave(role, s):
        pr, pi = waves[role, s, 0], waves[role, s, 1]
        o_r, o_i = patch[role, s, 0], patch[role, s, 1]
        return jnp.concatenate([pr * o_r - pi * o_i, pr * o_i + pi * o_r], 1)

    def stack(z):
        return jnp.concatenate([z[:, :n], z[:, n:]], 0)

    def step_top(s):
        z = right_mul(exit_wave(0, s), t_h[...], t_l[...])
        y = left_mul(k_h[...], k_l[...], stack(z))
        waves[0, s + 1, 0] = y[:n]
        waves[0, s + 1, 1] = y[n:]

    def edge_top(s):
        e = edge_term(0, s)
        for ri in range(2):
            waves[0, s + 1, ri, n - EDGE :] += e[ri * EDGE : (ri + 1) * EDGE]

    def step_bottom(s):
        await_patch(1, s)
        add_strip(1, s)
        z = right_mul(exit_wave(1, s), t_h[...], t_l[...])
        send_edge(0, s, z)
        y = left_mul(kb_h[...], kb_l[...], stack(z))
        waves[1, s + 1, 0] = y[:n]
        waves[1, s + 1, 1] = y[n:]

    row = row_off[q]
    kr, ki = masked(near, cr, ci)
    embed(t_h, t_l, *masked(near, er, ei))
    embed(k_h, k_l, kr, ki)
    edge_matrix(0, cr[n - EDGE :, :128], ci[n - EDGE :, :128])
    edge_matrix(
        1, pltpu.roll(er[:EDGE, n - 128 :], EDGE, 1), pltpu.roll(ei[:EDGE, n - 128 :], EDGE, 1)
    )
    for copy in small:
        copy.wait()
    for ri in range(2):
        waves[0, 0, ri] = pltpu.roll(probe[ri], row, 0)
    step_top(0)

    for copy in prev_copies:
        copy.wait()
    cut_role(1, prev_row, prev_col)
    send_role(1)
    for k, src in enumerate((row_off, prev_row, col_off, prev_col)):
        places[2 * k] = src[q]
        places[2 * k + 1] = src[oth]

    back = prev_row[q]
    embed(kb_h, kb_l, *masked(cut_mask(back), cr, ci))
    for ri in range(2):
        waves[1, 0, ri] = pltpu.roll(probe[ri], back, 0)

    def complex_left(high, low, x):
        w = x.shape[1] // 2
        out = left_mul(high, low, x)
        return out[:n, :w] - out[n:, w:], out[:n, w:] + out[n:, :w]

    qr, qi = complex_left(wh[...], wl[...], jnp.concatenate([kr, ki], 1))
    nr, ni = qr.T, qi.T
    for k in range(CHUNKS):
        c = slice(k * width, (k + 1) * width)
        put(n_h, n_l, (k, slice(0, n), slice(0, width)), nr[:, c])
        put(n_h, n_l, (k, slice(0, n), slice(width, 2 * width)), ni[:, c])
        put(n_h, n_l, (k, slice(n, 2 * n), slice(0, width)), -ni[:, c])
        put(n_h, n_l, (k, slice(n, 2 * n), slice(width, 2 * width)), nr[:, c])
        put(q_h, q_l, (k, slice(0, width), slice(0, n)), qr[c])
        put(q_h, q_l, (k, slice(0, width), slice(n, 2 * n)), -qi[c])
        put(q_h, q_l, (k, slice(width, 2 * width), slice(0, n)), qi[c])
        put(q_h, q_l, (k, slice(width, 2 * width), slice(n, 2 * n)), qr[c])

    def x_copy(k):
        return remote(x_out.at[k], x_in.at[k], sem_x_s.at[k], sem_x_r.at[k], prv, q)

    def y_copy(k):
        return remote(y_out.at[k], y_in.at[k], sem_y_s.at[k], sem_y_r.at[k], nxt, q)

    step_bottom(0)
    for s in range(1, last):
        step_bottom(s)
    await_patch(1, last)
    u = exit_wave(1, last)
    for k in range(CHUNKS):
        x_out[k] = right_mul(u, n_h[k], n_l[k])
        if k == 0:
            x_copy(k).start()

    for s in range(1, last):
        edge_top(s - 1)
        step_top(s)
        if s < CHUNKS:
            x_copy(s - 1).wait_send()
            x_copy(s).start()
    put(m_h, m_l, slice(0, n), pltpu.roll(qr, row, 1))
    put(m_h, m_l, slice(n, 2 * n), pltpu.roll(qi, row, 1))
    put(g_h, g_l, slice(0, n), pltpu.roll(nr, row, 0))
    put(g_h, g_l, slice(n, 2 * n), pltpu.roll(-ni, row, 0))
    embed(tt_h, tt_l, *masked(cut_mask(row), er, ei))
    edge_top(last - 1)
    await_patch(0, last)
    u = exit_wave(0, last)
    for k in range(CHUNKS):
        x_own[k] = right_mul(u, n_h[k], n_l[k])

    for k in range(CHUNKS):
        x_copy(k).wait_recv()
        x = jnp.where(row_index[:, : 2 * width] >= row, x_own[k], x_in[k])
        fr, fi = complex_left(m_h[...], m_l[...], x)
        residual = 2.0 * (fr * fr + fi * fi - intensity[:, k * width : (k + 1) * width])
        g = jnp.concatenate([residual * fr, residual * fi], 1)
        yr, yi = complex_left(g_h[...], g_l[...], g)
        y_out[k] = jnp.concatenate([yr, yi], 1)
        y_copy(k).start()
        if k == 0:
            x_copy(CHUNKS - 1).wait_send()
            for s in group[1]:
                strip_copy(1, s).start()

    def mine_copy(role, d):
        return pltpu.make_async_copy(
            terms.at[role, q * depth + d], mine.at[role, d], sem_mine.at[role, d]
        )

    def term_copy(role, d):
        return remote(
            terms.at[role, oth * depth + d], theirs.at[role, d],
            sem_term_s.at[role, d], sem_term_r.at[role, d], p, oth,
        )

    def finish(role, s, a_r, a_i):
        w_r, w_i = waves[role, s, 0], waves[role, s, 1]
        terms[role, s, 0] = a_r * w_r + a_i * w_i
        terms[role, s, 1] = a_i * w_r - a_r * w_i
        if s > 0:
            o_r, o_i = patch[role, s, 0], patch[role, s, 1]
            if role == 1:
                o_r, o_i = masked(row_index < back, o_r, o_i)
            chi[role, 0] = a_r * o_r + a_i * o_i
            chi[role, 1] = a_i * o_r - a_r * o_i

        @pl.when(q == s // depth)
        def _():
            mine_copy(role, s % depth).start()

        @pl.when(q != s // depth)
        def _():
            term_copy(role, s % depth).start()

    def backward_right(x):
        return right_mul(x, k_h[...], k_l[...])

    for role in range(2):
        a = jnp.zeros((n, 2 * n), F32)
        for k in range(CHUNKS):
            if role == 1:
                y_copy(k).wait_recv()
            a += right_mul((y_out, y_in)[role][k], q_h[k], q_l[k])
        a_r, a_i = a[:, :n], a[:, n:]
        finish(role, last, a_r, a_i)
        for s in range(last - 1, -1, -1):
            z = backward_right(jnp.concatenate([chi[role, 0], chi[role, 1]], 1))
            if role == 0:
                send_edge(1, s, z)
                rows = extent[1][s + 1]
                strip_copy(1, s + 1).wait_recv()
                s_r, s_i = strips[0, s + 1, 0, :rows], strips[0, s + 1, 1, :rows]
                b_r, b_i = a_r[:rows], a_i[:rows]
                margin = jnp.concatenate([b_r * s_r + b_i * s_i, b_i * s_r - b_r * s_i], 1)
                z = jnp.concatenate([z[:rows] + backward_right(margin), z[rows:]], 0)
                y = left_mul(tt_h[...], tt_l[...], stack(z))
            else:
                y = left_mul(t_h[...], t_l[...], stack(z))
                e = edge_term(1, s)
                y = jnp.concatenate(
                    [y[:EDGE] + e[:EDGE], y[EDGE:n], y[n : n + EDGE] + e[EDGE:], y[n + EDGE :]], 0
                )
            a_r, a_i = y[:n], y[n:]
            finish(role, s, a_r, a_i)

    for role in range(2):
        for d in range(depth):
            patch_copy(role, d, q).wait_send()
        for s in group[role]:
            strip_copy(role, s).wait_send()
        for s in range(last):
            edge_copy(role, s).wait_send()
    for k in range(CHUNKS):
        y_copy(k).wait_send()
    for role in range(2):
        for d in range(depth):
            mine_copy(role, d).wait()
            term_copy(role, d).wait()


def column_place(col, cols_all, span):
    base = jnp.minimum(col // 128 * 128, cols_all - span)
    return pl.multiple_of(base, 128), col - base


def deposit_kernel(places, mine, theirs, out_r, out_i):
    rows, n = mine.shape[-2:]
    span = n + 128
    row_index = lax.broadcasted_iota(jnp.int32, (rows, n), 0) + pl.program_id(1) * rows
    lane_index = lax.broadcasted_iota(jnp.int32, (rows, 128), 1)
    for ri, out in enumerate((out_r, out_i)):
        out[...] = jnp.zeros_like(out)
        for k in range(4):
            role, src = k // 2, (mine, theirs)[k % 2]
            row, col = places[k], places[4 + k]
            keep = row_index >= row if role == 0 else row_index < row
            term = jnp.where(keep, src[role, 0, ri], 0.0)
            base, shift = column_place(col, out.shape[-1], span)
            zero = jnp.zeros((rows, 128), F32)
            turned = [
                pltpu.roll(term[:, b : b + 128], lax.rem(shift, 128), 1) for b in range(0, n, 128)
            ]
            right = lane_index >= shift
            wide = jnp.concatenate(
                [jnp.where(right, a, b) for a, b in zip(turned + [zero], [zero] + turned)], 1
            )
            out[0, :, pl.ds(base, span)] += wide


def local(obj_real, obj_imag, probe, taps, intensity, row_off, col_off):
    n = probe.shape[-1]
    depth, tile, cols_all = obj_real.shape
    slices = 2 * depth
    wide = 2 * n // CHUNKS
    longest = max(max(strip_rows(slices, (taps.shape[1] - 1) // 2)))
    dma = pltpu.SemaphoreType.DMA
    terms = jax.ShapeDtypeStruct((2, depth, 2, n, n), F32)
    half_obj = pltpu.VMEM((2, cols_all // 128, tile, 128), F32)
    windows = pltpu.VMEM((2, slices, 2, n, n), F32)
    mine, theirs, places = pl.pallas_call(
        fused_kernel,
        out_shape=[terms, terms, jax.ShapeDtypeStruct((8,), jnp.int32)],
        in_specs=[ANY, ANY, ANY, VMEM, ANY, SMEM, SMEM, ANY, ANY],
        out_specs=[ANY, ANY, SMEM],
        scratch_shapes=[
            half_obj, half_obj,
            pltpu.VMEM((2, n, n), F32),
            pltpu.VMEM((n, n), F32),
            pltpu.VMEM((2 * n, n), BF16),
            pltpu.VMEM((2 * n, n), BF16),
            windows,
            pltpu.VMEM((2, depth, 2, n, n), F32),
            pltpu.VMEM((2, slices, 2, longest, n), F32),
            windows,
            pltpu.VMEM((2, 2, n, n), F32),
            windows,
        ]
        + [pltpu.VMEM((CHUNKS, n, wide), F32)] * 5
        + [pltpu.VMEM((8, n), F32)]
        + [pltpu.SMEM((2,), jnp.int32)] * 2
        + [pltpu.VMEM((2 * n, 2 * n), BF16)] * 8
        + [pltpu.VMEM((2 * n, n), BF16)] * 4
        + [pltpu.VMEM((CHUNKS, 2 * n, wide), BF16)] * 2
        + [pltpu.VMEM((CHUNKS, wide, 2 * n), BF16)] * 2
        + [pltpu.VMEM((2, slices - 1, 2, EDGE, n), F32)] * 2
        + [pltpu.VMEM((2, 2 * EDGE, 8 * EDGE), BF16)]
        + [
            dma((2, depth, cols_all // 128)), dma((4,)), dma((2,)), dma((2,)),
            dma((2, depth)), dma((2, depth)), dma((2, slices)), dma((2, slices)),
            dma((2, slices - 1)), dma((2, slices - 1)),
            dma((CHUNKS,)), dma((CHUNKS,)), dma((CHUNKS,)), dma((CHUNKS,)),
            dma((2, depth)), dma((2, depth)), dma((2, depth)),
        ],
        compiler_params=pltpu.CompilerParams(
            collective_id=0, has_side_effects=True, vmem_limit_bytes=60 * 2**20
        ),
        name="fused",
    )(obj_real, obj_imag, probe, taps, intensity, row_off, col_off, *fourier_left(n))

    terms_spec = pl.BlockSpec((2, 1, 2, n // PIECES, n), lambda d, h: (0, d, 0, h, 0))
    plane_spec = pl.BlockSpec((1, tile // PIECES, cols_all), lambda d, h: (d, h, 0))
    return pl.pallas_call(
        deposit_kernel,
        grid=(depth, PIECES),
        out_shape=[jax.ShapeDtypeStruct(obj_real.shape, F32)] * 2,
        in_specs=[SMEM, terms_spec, terms_spec],
        out_specs=[plane_spec] * 2,
        compiler_params=pltpu.CompilerParams(vmem_limit_bytes=60 * 2**20),
        name="deposit",
    )(places, mine, theirs)


def solution(mesh):
    in_specs = (
        P(("parts", "slab"), "pos", None),
        P(("parts", "slab"), "pos", None),
        P(),
        P(),
        P(("parts", "pos"), None, None),
        P(("parts", "pos")),
        P(("parts", "pos")),
    )
    out_specs = (P(("parts", "slab"), "pos", None), P(("parts", "slab"), "pos", None))
    return jax.shard_map(local, mesh=mesh, in_specs=in_specs, out_specs=out_specs, check_vma=False)
```

```python
import functools
import math

import jax
import jax.numpy as jnp
import numpy as np
from jax import lax
from jax.experimental import pallas as pl
from jax.experimental.pallas import tpu as pltpu
from jax.sharding import PartitionSpec as P

F32 = jnp.float32
BF16 = jnp.bfloat16
SMEM = pl.BlockSpec(memory_space=pltpu.SMEM)
VMEM = pl.BlockSpec(memory_space=pltpu.VMEM)
ANY = pl.BlockSpec(memory_space=pl.ANY)
CHUNKS = 2
EDGE = 32
PIECES = 1


def halves(x):
    high = x.astype(BF16)
    return high, (x - high.astype(F32)).astype(BF16)


def left_mul(high, low, x):
    xh, xl = halves(x)
    left = jnp.concatenate([high, high, low], 1)
    right = jnp.concatenate([xh, xl, xh], 0)
    return jnp.dot(left, right, preferred_element_type=F32)


def right_mul(x, high, low):
    xh, xl = halves(x)
    left = jnp.concatenate([xh, xl, xh], 1)
    right = jnp.concatenate([high, high, low], 0)
    return jnp.dot(left, right, preferred_element_type=F32)


def fourier_left(n):
    steps = np.arange(n)
    angle = 2.0 * math.pi / n * ((steps[:, None] * steps[None, :]) % n)
    norm = 1.0 / math.sqrt(n)
    m = np.concatenate([np.cos(angle) * norm, -np.sin(angle) * norm], 0).astype(np.float32)
    high = m.astype(jnp.bfloat16)
    return jnp.asarray(high), jnp.asarray((m - high.astype(np.float32)).astype(jnp.bfloat16))


def put(high, low, at, block):
    hi, lo = halves(block)
    high[at] = hi
    low[at] = lo


def embed(high, low, re, im):
    n = re.shape[0]
    one, two = slice(0, n), slice(n, 2 * n)
    for ref, r, i in zip((high, low), halves(re), halves(im)):
        ref[one, one] = r
        ref[one, two] = -i
        ref[two, one] = i
        ref[two, two] = r


def strip_rows(slices, half):
    forward = [half * (slices - 1 - s) for s in range(slices)]
    backward = [half * s for s in range(slices)]
    return [[-(-rows // 8) * 8 for rows in need] for need in (forward, backward)]


def fused_kernel(
    obj_r, obj_i, probe_any, taps, intensity_any, row_off, col_off, wh_any, wl_any,
    mine, theirs, places,
    obj_0, obj_1, probe, intensity, wh, wl, patch, outbound, strips, waves, chi, terms,
    x_out, x_in, x_own, y_out, y_in, ring, prev_row, prev_col,
    k_h, k_l, t_h, t_l, kb_h, kb_l, tt_h, tt_l,
    m_h, m_l, g_h, g_l, n_h, n_l, q_h, q_l, edge_out, edge_in, edge_m,
    sem_obj, sem_in, sem_prev_s, sem_prev_r, sem_patch_s, sem_patch_r, sem_strip_s, sem_strip_r,
    sem_edge_s, sem_edge_r, sem_x_s, sem_x_r, sem_y_s, sem_y_r, sem_mine, sem_term_s, sem_term_r,
):
    n = probe.shape[-1]
    obj_v = (obj_0, obj_1)
    depth = len(obj_v)
    slices = 2 * depth
    last = slices - 1
    width = n // CHUNKS
    span = n + 128
    taps_count = taps.shape[1]
    half = (taps_count - 1) // 2
    extent = strip_rows(slices, half)
    p, q = lax.axis_index("pos"), lax.axis_index("slab")
    npos = lax.axis_size("pos")
    nxt, prv, oth = lax.rem(p + 1, npos), lax.rem(p + npos - 1, npos), 1 - q

    def remote(src, dst, send, recv, pos, slab):
        return pltpu.make_async_remote_copy(
            src_ref=src, dst_ref=dst, send_sem=send, recv_sem=recv,
            device_id={"pos": pos, "slab": slab}, device_id_type=pl.DeviceIdType.MESH,
        )

    blocks = obj_0.shape[1]

    def obj_copies(d):
        return [
            pltpu.make_async_copy(
                src.at[d, :, pl.ds(b * 128, 128)], obj_v[d].at[ri, b], sem_obj.at[ri, d, b]
            )
            for ri, src in enumerate((obj_r, obj_i))
            for b in range(blocks)
        ]

    for d in range(depth):
        for copy in obj_copies(d):
            copy.start()
    small = [
        pltpu.make_async_copy(src, dst, sem_in.at[k])
        for k, (src, dst) in enumerate(
            ((wh_any, wh), (wl_any, wl), (probe_any, probe), (intensity_any.at[q], intensity))
        )
    ]
    for copy in small:
        copy.start()

    barrier = pltpu.get_barrier_semaphore()
    for pos, slab in ((nxt, q), (prv, q), (p, oth)):
        pl.semaphore_signal(
            barrier, inc=1, device_id={"pos": pos, "slab": slab},
            device_id_type=pl.DeviceIdType.MESH,
        )

    row_index = lax.broadcasted_iota(jnp.int32, (n, n), 0)
    col_index = lax.broadcasted_iota(jnp.int32, (n, n), 1)
    near = jnp.abs(row_index - col_index) < n // 2
    lane_index = lax.broadcasted_iota(jnp.int32, (n, 128), 1)

    def cut(dst, d, row, col, role):
        keep = row_index >= row if role == 0 else row_index < row
        first = jnp.minimum(col // 128, blocks - span // 128)
        shift = col - first * 128
        left = lane_index < 128 - shift
        for ri in range(2):
            turned = [
                pltpu.roll(obj_v[d][ri, first + b], lax.rem(128 - shift, 128), 1)
                for b in range(span // 128)
            ]
            part = jnp.concatenate(
                [jnp.where(left, a, b) for a, b in zip(turned[:-1], turned[1:])], 1
            )
            dst[ri] = jnp.where(keep, part, 0.0)

    def patch_copy(role, d, owner):
        return remote(
            outbound.at[role, d], patch.at[role, owner * depth + d],
            sem_patch_s.at[role, d], sem_patch_r.at[role, d], p, oth,
        )

    def strip_copy(role, s):
        rows = extent[role][s]
        at = pl.ds(n - rows, rows) if role == 0 else pl.ds(0, rows)
        return remote(
            patch.at[role, s, :, at], strips.at[1 - role, s, :, pl.ds(0, rows)],
            sem_strip_s.at[role, s], sem_strip_r.at[1 - role, s], (nxt, prv)[role], q,
        )

    def await_patch(role, s):
        @pl.when(q != s // depth)
        def _():
            patch_copy(role, s % depth, oth).wait_recv()

    group = (tuple(range(last)), tuple(range(last, 0, -1)))

    def cut_role(role, rows, cols):
        for d in range(depth):
            if role == 0:
                for copy in obj_copies(d):
                    copy.wait()
            cut(outbound.at[role, d], d, rows[oth], cols[oth], role)
            cut(patch.at[role, q * depth + d], d, rows[q], cols[q], role)

    def send_role(role):
        for d in range(depth):
            patch_copy(role, d, q).start()

    cut_role(0, row_off, col_off)
    pl.semaphore_wait(barrier, 3)
    prev_copies = [
        remote(src, dst, sem_prev_s.at[k], sem_prev_r.at[k], nxt, q)
        for k, (src, dst) in enumerate(((row_off, prev_row), (col_off, prev_col)))
    ]
    for copy in prev_copies:
        copy.start()
    send_role(0)
    for s in group[0]:
        await_patch(0, s)
        strip_copy(0, s).start()

    ring[...] = jnp.zeros_like(ring)
    ring[:2, :taps_count] = taps[...]
    tap = pltpu.roll(ring[...], n - half, 1)

    def circulant(k):
        rows = jnp.broadcast_to(tap[k : k + 1, :], (n, n))
        return pltpu.roll(rows, 0, 1, stride=1, stride_axis=0)

    cr, ci = circulant(0), circulant(1)
    er, ei = cr.T, -ci.T

    def masked(keep, re, im):
        return jnp.where(keep, re, 0.0), jnp.where(keep, im, 0.0)

    def cut_mask(row):
        return ((row_index < row) == (col_index < row)) == near

    def edge_matrix(at, re, im):
        top = re + pltpu.roll(-im, EDGE, 1)
        bottom = im + pltpu.roll(re, EDGE, 1)
        both = jnp.concatenate([top, bottom], 0)
        high = both.astype(BF16).astype(F32)
        edge_m[at, :, :128] = (high + pltpu.roll(high, 2 * EDGE, 1)).astype(BF16)
        edge_m[at, :, 128:] = (both - high).astype(BF16)

    def edge_copy(way, step):
        return remote(
            edge_out.at[way, step], edge_in.at[way, step],
            sem_edge_s.at[way, step], sem_edge_r.at[way, step], (prv, nxt)[way], q,
        )

    def send_edge(way, step, z):
        at = slice(0, EDGE) if way == 0 else slice(n - EDGE, n)
        for ri in range(2):
            edge_out[way, step, ri] = z[at, ri * n : (ri + 1) * n]
        edge_copy(way, step).start()

    def edge_term(way, step):
        edge_copy(way, step).wait_recv()
        xh, xl = halves(jnp.concatenate([edge_in[way, step, 0], edge_in[way, step, 1]], 0))
        right = jnp.concatenate([xh, xl, xh, jnp.zeros_like(xh)], 0)
        return jnp.dot(edge_m[way], right, preferred_element_type=F32)

    def add_strip(role, s):
        rows = extent[1 - role][s]
        strip_copy(1 - role, s).wait_recv()
        for ri in range(2):
            patch[role, s, ri, n - rows :] += strips[role, s, ri, :rows]

    def exit_wave(role, s):
        pr, pi = waves[role, s, 0], waves[role, s, 1]
        o_r, o_i = patch[role, s, 0], patch[role, s, 1]
        return jnp.concatenate([pr * o_r - pi * o_i, pr * o_i + pi * o_r], 1)

    def stack(z):
        return jnp.concatenate([z[:, :n], z[:, n:]], 0)

    def step_top(s):
        z = right_mul(exit_wave(0, s), t_h[...], t_l[...])
        y = left_mul(k_h[...], k_l[...], stack(z))
        waves[0, s + 1, 0] = y[:n]
        waves[0, s + 1, 1] = y[n:]

    def edge_top(s):
        e = edge_term(0, s)
        for ri in range(2):
            waves[0, s + 1, ri, n - EDGE :] += e[ri * EDGE : (ri + 1) * EDGE]

    def step_bottom(s):
        await_patch(1, s)
        add_strip(1, s)
        z = right_mul(exit_wave(1, s), t_h[...], t_l[...])
        send_edge(0, s, z)
        y = left_mul(kb_h[...], kb_l[...], stack(z))
        waves[1, s + 1, 0] = y[:n]
        waves[1, s + 1, 1] = y[n:]

    row = row_off[q]
    kr, ki = masked(near, cr, ci)
    embed(t_h, t_l, *masked(near, er, ei))
    embed(k_h, k_l, kr, ki)
    edge_matrix(0, cr[n - EDGE :, :128], ci[n - EDGE :, :128])
    edge_matrix(
        1, pltpu.roll(er[:EDGE, n - 128 :], EDGE, 1), pltpu.roll(ei[:EDGE, n - 128 :], EDGE, 1)
    )
    for copy in small:
        copy.wait()
    for ri in range(2):
        waves[0, 0, ri] = pltpu.roll(probe[ri], row, 0)
    for copy in prev_copies:
        copy.wait()
    cut_role(1, prev_row, prev_col)
    send_role(1)
    for k, src in enumerate((row_off, prev_row, col_off, prev_col)):
        places[2 * k] = src[q]
        places[2 * k + 1] = src[oth]

    back = prev_row[q]
    embed(kb_h, kb_l, *masked(cut_mask(back), cr, ci))
    for ri in range(2):
        waves[1, 0, ri] = pltpu.roll(probe[ri], back, 0)

    def complex_left(high, low, x):
        w = x.shape[1] // 2
        out = left_mul(high, low, x)
        return out[:n, :w] - out[n:, w:], out[:n, w:] + out[n:, :w]

    qr, qi = complex_left(wh[...], wl[...], jnp.concatenate([kr, ki], 1))
    nr, ni = qr.T, qi.T
    for k in range(CHUNKS):
        c = slice(k * width, (k + 1) * width)
        put(n_h, n_l, (k, slice(0, n), slice(0, width)), nr[:, c])
        put(n_h, n_l, (k, slice(0, n), slice(width, 2 * width)), ni[:, c])
        put(n_h, n_l, (k, slice(n, 2 * n), slice(0, width)), -ni[:, c])
        put(n_h, n_l, (k, slice(n, 2 * n), slice(width, 2 * width)), nr[:, c])
        put(q_h, q_l, (k, slice(0, width), slice(0, n)), qr[c])
        put(q_h, q_l, (k, slice(0, width), slice(n, 2 * n)), -qi[c])
        put(q_h, q_l, (k, slice(width, 2 * width), slice(0, n)), qi[c])
        put(q_h, q_l, (k, slice(width, 2 * width), slice(n, 2 * n)), qr[c])

    step_top(0)

    def x_copy(k):
        return remote(x_out.at[k], x_in.at[k], sem_x_s.at[k], sem_x_r.at[k], prv, q)

    def y_copy(k):
        return remote(y_out.at[k], y_in.at[k], sem_y_s.at[k], sem_y_r.at[k], nxt, q)

    step_bottom(0)
    for s in range(1, last):
        step_bottom(s)
    await_patch(1, last)
    u = exit_wave(1, last)
    for k in range(CHUNKS):
        x_out[k] = right_mul(u, n_h[k], n_l[k])
        if k == 0:
            x_copy(k).start()

    for s in range(1, last):
        edge_top(s - 1)
        step_top(s)
        if s < CHUNKS:
            x_copy(s - 1).wait_send()
            x_copy(s).start()
    put(m_h, m_l, slice(0, n), pltpu.roll(qr, row, 1))
    put(m_h, m_l, slice(n, 2 * n), pltpu.roll(qi, row, 1))
    put(g_h, g_l, slice(0, n), pltpu.roll(nr, row, 0))
    put(g_h, g_l, slice(n, 2 * n), pltpu.roll(-ni, row, 0))
    embed(tt_h, tt_l, *masked(cut_mask(row), er, ei))
    edge_top(last - 1)
    await_patch(0, last)
    u = exit_wave(0, last)
    for k in range(CHUNKS):
        x_own[k] = right_mul(u, n_h[k], n_l[k])

    for k in range(CHUNKS):
        x_copy(k).wait_recv()
        x = jnp.where(row_index[:, : 2 * width] >= row, x_own[k], x_in[k])
        fr, fi = complex_left(m_h[...], m_l[...], x)
        residual = 2.0 * (fr * fr + fi * fi - intensity[:, k * width : (k + 1) * width])
        g = jnp.concatenate([residual * fr, residual * fi], 1)
        yr, yi = complex_left(g_h[...], g_l[...], g)
        y_out[k] = jnp.concatenate([yr, yi], 1)
        y_copy(k).start()
        if k == 0:
            x_copy(CHUNKS - 1).wait_send()
            for s in group[1]:
                strip_copy(1, s).start()

    def mine_copy(role, d):
        return pltpu.make_async_copy(
            terms.at[role, q * depth + d], mine.at[role, d], sem_mine.at[role, d]
        )

    def term_copy(role, d):
        return remote(
            terms.at[role, oth * depth + d], theirs.at[role, d],
            sem_term_s.at[role, d], sem_term_r.at[role, d], p, oth,
        )

    def finish(role, s, a_r, a_i):
        w_r, w_i = waves[role, s, 0], waves[role, s, 1]
        terms[role, s, 0] = a_r * w_r + a_i * w_i
        terms[role, s, 1] = a_i * w_r - a_r * w_i
        if s > 0:
            o_r, o_i = patch[role, s, 0], patch[role, s, 1]
            if role == 1:
                o_r, o_i = masked(row_index < back, o_r, o_i)
            chi[role, 0] = a_r * o_r + a_i * o_i
            chi[role, 1] = a_i * o_r - a_r * o_i

        @pl.when(q == s // depth)
        def _():
            mine_copy(role, s % depth).start()

        @pl.when(q != s // depth)
        def _():
            term_copy(role, s % depth).start()

    def backward_right(x):
        return right_mul(x, k_h[...], k_l[...])

    for role in range(2):
        a = jnp.zeros((n, 2 * n), F32)
        for k in range(CHUNKS):
            if role == 1:
                y_copy(k).wait_recv()
            a += right_mul((y_out, y_in)[role][k], q_h[k], q_l[k])
        a_r, a_i = a[:, :n], a[:, n:]
        finish(role, last, a_r, a_i)
        for s in range(last - 1, -1, -1):
            z = backward_right(jnp.concatenate([chi[role, 0], chi[role, 1]], 1))
            if role == 0:
                send_edge(1, s, z)
                rows = extent[1][s + 1]
                strip_copy(1, s + 1).wait_recv()
                s_r, s_i = strips[0, s + 1, 0, :rows], strips[0, s + 1, 1, :rows]
                b_r, b_i = a_r[:rows], a_i[:rows]
                margin = jnp.concatenate([b_r * s_r + b_i * s_i, b_i * s_r - b_r * s_i], 1)
                z = jnp.concatenate([z[:rows] + backward_right(margin), z[rows:]], 0)
                y = left_mul(tt_h[...], tt_l[...], stack(z))
            else:
                y = left_mul(t_h[...], t_l[...], stack(z))
                e = edge_term(1, s)
                y = jnp.concatenate(
                    [y[:EDGE] + e[:EDGE], y[EDGE:n], y[n : n + EDGE] + e[EDGE:], y[n + EDGE :]], 0
                )
            a_r, a_i = y[:n], y[n:]
            finish(role, s, a_r, a_i)

    for role in range(2):
        for d in range(depth):
            patch_copy(role, d, q).wait_send()
        for s in group[role]:
            strip_copy(role, s).wait_send()
        for s in range(last):
            edge_copy(role, s).wait_send()
    for k in range(CHUNKS):
        y_copy(k).wait_send()
    for role in range(2):
        for d in range(depth):
            mine_copy(role, d).wait()
            term_copy(role, d).wait()


def column_place(col, cols_all, span):
    base = jnp.minimum(col // 128 * 128, cols_all - span)
    return pl.multiple_of(base, 128), col - base


def deposit_kernel(places, mine, theirs, out_r, out_i):
    rows, n = mine.shape[-2:]
    span = n + 128
    row_index = lax.broadcasted_iota(jnp.int32, (rows, n), 0) + pl.program_id(1) * rows
    lane_index = lax.broadcasted_iota(jnp.int32, (rows, 128), 1)
    for ri, out in enumerate((out_r, out_i)):
        out[...] = jnp.zeros_like(out)
        for k in range(4):
            role, src = k // 2, (mine, theirs)[k % 2]
            row, col = places[k], places[4 + k]
            keep = row_index >= row if role == 0 else row_index < row
            term = jnp.where(keep, src[role, 0, ri], 0.0)
            base, shift = column_place(col, out.shape[-1], span)
            zero = jnp.zeros((rows, 128), F32)
            turned = [
                pltpu.roll(term[:, b : b + 128], lax.rem(shift, 128), 1) for b in range(0, n, 128)
            ]
            right = lane_index >= shift
            wide = jnp.concatenate(
                [jnp.where(right, a, b) for a, b in zip(turned + [zero], [zero] + turned)], 1
            )
            out[0, :, pl.ds(base, span)] += wide


def local(obj_real, obj_imag, probe, taps, intensity, row_off, col_off):
    n = probe.shape[-1]
    depth, tile, cols_all = obj_real.shape
    slices = 2 * depth
    wide = 2 * n // CHUNKS
    longest = max(max(strip_rows(slices, (taps.shape[1] - 1) // 2)))
    dma = pltpu.SemaphoreType.DMA
    terms = jax.ShapeDtypeStruct((2, depth, 2, n, n), F32)
    half_obj = pltpu.VMEM((2, cols_all // 128, tile, 128), F32)
    windows = pltpu.VMEM((2, slices, 2, n, n), F32)
    mine, theirs, places = pl.pallas_call(
        fused_kernel,
        out_shape=[terms, terms, jax.ShapeDtypeStruct((8,), jnp.int32)],
        in_specs=[ANY, ANY, ANY, VMEM, ANY, SMEM, SMEM, ANY, ANY],
        out_specs=[ANY, ANY, SMEM],
        scratch_shapes=[
            half_obj, half_obj,
            pltpu.VMEM((2, n, n), F32),
            pltpu.VMEM((n, n), F32),
            pltpu.VMEM((2 * n, n), BF16),
            pltpu.VMEM((2 * n, n), BF16),
            windows,
            pltpu.VMEM((2, depth, 2, n, n), F32),
            pltpu.VMEM((2, slices, 2, longest, n), F32),
            windows,
            pltpu.VMEM((2, 2, n, n), F32),
            windows,
        ]
        + [pltpu.VMEM((CHUNKS, n, wide), F32)] * 5
        + [pltpu.VMEM((8, n), F32)]
        + [pltpu.SMEM((2,), jnp.int32)] * 2
        + [pltpu.VMEM((2 * n, 2 * n), BF16)] * 8
        + [pltpu.VMEM((2 * n, n), BF16)] * 4
        + [pltpu.VMEM((CHUNKS, 2 * n, wide), BF16)] * 2
        + [pltpu.VMEM((CHUNKS, wide, 2 * n), BF16)] * 2
        + [pltpu.VMEM((2, slices - 1, 2, EDGE, n), F32)] * 2
        + [pltpu.VMEM((2, 2 * EDGE, 8 * EDGE), BF16)]
        + [
            dma((2, depth, cols_all // 128)), dma((4,)), dma((2,)), dma((2,)),
            dma((2, depth)), dma((2, depth)), dma((2, slices)), dma((2, slices)),
            dma((2, slices - 1)), dma((2, slices - 1)),
            dma((CHUNKS,)), dma((CHUNKS,)), dma((CHUNKS,)), dma((CHUNKS,)),
            dma((2, depth)), dma((2, depth)), dma((2, depth)),
        ],
        compiler_params=pltpu.CompilerParams(
            collective_id=0, has_side_effects=True, vmem_limit_bytes=60 * 2**20
        ),
        name="fused",
    )(obj_real, obj_imag, probe, taps, intensity, row_off, col_off, *fourier_left(n))

    terms_spec = pl.BlockSpec((2, 1, 2, n // PIECES, n), lambda d, h: (0, d, 0, h, 0))
    plane_spec = pl.BlockSpec((1, tile // PIECES, cols_all), lambda d, h: (d, h, 0))
    return pl.pallas_call(
        deposit_kernel,
        grid=(depth, PIECES),
        out_shape=[jax.ShapeDtypeStruct(obj_real.shape, F32)] * 2,
        in_specs=[SMEM, terms_spec, terms_spec],
        out_specs=[plane_spec] * 2,
        compiler_params=pltpu.CompilerParams(vmem_limit_bytes=60 * 2**20),
        name="deposit",
    )(places, mine, theirs)


def solution(mesh):
    in_specs = (
        P(("parts", "slab"), "pos", None),
        P(("parts", "slab"), "pos", None),
        P(),
        P(),
        P(("parts", "pos"), None, None),
        P(("parts", "pos")),
        P(("parts", "pos")),
    )
    out_specs = (P(("parts", "slab"), "pos", None), P(("parts", "slab"), "pos", None))
    return jax.shard_map(local, mesh=mesh, in_specs=in_specs, out_specs=out_specs, check_vma=False)
```
